256 devices in a mesh: dom: 32 (over z, y), samp: 8 (over x, core).
Axes of the slice: x: 4, y: 4, z: 8, core: 2. Of those that a mesh axis runs over, the one named last changes fastest.
Arguments:
- residual: float32 [256, 131072], P('samp', 'dom'), may hold values from -60 to 60
- conductance: float32 [256, 131072], P('samp', 'dom'), may hold values from 0.2 to 2
- capacitance: float32 [256, 131072], P('samp', 'dom'), may hold values from 0.2 to 2
- stamps: float32 [2048, 4, 64, 128], P('dom'), may hold values from -0.375 to 0.375
- block_cols: int32 [2048, 4], P('dom'), may hold values from 0 to 191, as said below
- send_blocks: int32 [32, 32, 4], P('dom'), may hold values from 0 to 63
Outputs:
- update: float32 [256, 131072], P('samp', 'dom')
The draws below stay inside these ranges and needn't reach their ends.
Inputs may be any that keep to these rules, and one draw needn't show every extreme that they name: `block_cols`: entries below 64 name the partition's own block rows; an entry 64 + s * 4 + j names slot j that partition s sends to this partition, s never the partition itself; entry 0 of a row is the row's own block.
All inputs are finite; a program needn't handle non-finite values.
Results may differ from the reference program's by a relative error of at most 0.00005.
Values sent between devices are 32-bit elements; how exact they have to be, the bound alone decides.
A program may use at most 64 MiB of HBM per device.

```python
import math
import jax
import jax.numpy as jnp
from jax import lax

BLK = 64
PER_ROW = 4
SLOTS = 4
SAMPLES = 256
ROWS_DEV = 64
BLOCKS = 2048
UNKNOWNS = 131072
N_DOM = 32


def draw_block_cols(key, part):
    domains = BLOCKS // ROWS_DEV
    rows = jnp.arange(BLOCKS, dtype=jnp.int32)
    owner = rows // ROWS_DEV
    local = rows % ROWS_DEV
    columns = [local]
    for entry in range(1, PER_ROW):
        keys = jax.random.split(jax.random.fold_in(key, entry), 4)
        position = local * (PER_ROW - 1) + (entry - 1)
        forced = position < domains - 1
        forced_value = ROWS_DEV + (owner + 1 + position) % domains * SLOTS + SLOTS - 1
        remote_flag = jax.random.randint(keys[0], (BLOCKS,), 0, 2)
        offset = jax.random.randint(keys[1], (BLOCKS,), 1, domains)
        slot = jax.random.randint(keys[2], (BLOCKS,), 0, SLOTS)
        near = jax.random.randint(keys[3], (BLOCKS,), 0, ROWS_DEV)
        random_far = ROWS_DEV + (owner + offset) % domains * SLOTS + slot
        chosen = jnp.where(remote_flag == 1, random_far, near)
        columns.append(jnp.where(forced, forced_value, chosen))
    return jnp.stack(columns, axis=1).astype(jnp.int32)


def draw_residual(key, part):
    keys = jax.random.split(jax.random.fold_in(key, 7), 3)
    ramp_rows = 1.0 + 2.0 * jnp.arange(SAMPLES, dtype=jnp.float32) / SAMPLES
    ramp_columns = 1.0 + 2.0 * jnp.arange(UNKNOWNS, dtype=jnp.float32) / UNKNOWNS
    row_scale = jnp.exp(jax.random.uniform(keys[0], (SAMPLES,), jnp.float32, 0.0, math.log(10.0))) * ramp_rows
    column_scale = jnp.exp(jax.random.uniform(keys[1], (UNKNOWNS,), jnp.float32, 0.0, math.log(10.0))) * ramp_columns
    base = jax.random.normal(keys[2], (SAMPLES, UNKNOWNS), jnp.float32)
    value = 0.3 * base * row_scale[:, None] * column_scale[None, :]
    return jnp.clip(value, -60.0, 60.0).astype(jnp.float32)


def plant(result, stream_key, smallest, high):
    longest = result.shape.index(max(result.shape))
    spots = []
    for shift in (0, 1):
        where = [jax.random.randint(jax.random.fold_in(stream_key, axis), (), 0, length) for axis, length in enumerate(result.shape)]
        where[longest] = (where[longest] + shift) % result.shape[longest]
        spots.append(tuple(where))
    return result.at[spots[0]].set(smallest).at[spots[1]].set(high)


def level_of(key, dims, cuts, low, largest):
    level = 1.0
    for axis_at, blocks in cuts:
        steps = jax.random.uniform(jax.random.fold_in(jax.random.fold_in(key, 6), axis_at), (blocks,), jnp.float32, low / len(cuts), largest / len(cuts))
        level = level * jnp.repeat(jnp.exp(steps), dims[axis_at] // blocks).reshape((-1,) + (1,) * (len(dims) - 1 - axis_at))
    return level


def centred(own_key, shape, deviation, limit, shards=(), kind=jnp.bfloat16):
    values = deviation * jax.random.normal(own_key, shape, jnp.float32)
    if shards:
        values = values * level_of(own_key, shape, shards, -0.22, 0.18)
    return jnp.clip(values, -limit, limit).astype(kind)


def setup_inputs(seed: int = 0) -> dict:
    splits = jax.random.split(jax.random.key(seed), 7)
    residual = draw_residual(jax.random.fold_in(splits[6], 71), 0)
    conductance = jnp.clip(jnp.exp(math.log(2.0) - 2.3025851 * jax.random.uniform(splits[1], (SAMPLES, UNKNOWNS), jnp.float32) ** level_of(splits[1], (SAMPLES, UNKNOWNS), ((0, 8), (1, 32)), -0.2, 0.2)), 0.2, 2.0)
    capacitance = jnp.clip(jnp.exp(math.log(2.0) - 2.3025851 * jax.random.uniform(splits[2], (SAMPLES, UNKNOWNS), jnp.float32) ** level_of(splits[2], (SAMPLES, UNKNOWNS), ((0, 8), (1, 32)), -0.2, 0.2)), 0.2, 2.0)
    stamps = centred(splits[3], (BLOCKS, PER_ROW, BLK, 2 * BLK), (PER_ROW * BLK) ** -0.5, 0.375, ((0, 32),), jnp.float32)
    block_cols = draw_block_cols(jax.random.fold_in(splits[6], 71), 0)
    send_blocks = plant(jax.random.randint(splits[5], (N_DOM, N_DOM, SLOTS), 0, ROWS_DEV), jax.random.fold_in(splits[5], 1), 0, ROWS_DEV - 1).astype(jnp.int32)
    return dict(residual=residual, conductance=conductance, capacitance=capacitance, stamps=stamps, block_cols=block_cols, send_blocks=send_blocks)


def spectral_block(first_row, rows, first_column, columns, order):
    row_ids = first_row + jnp.arange(rows, dtype=jnp.int32)
    column_ids = first_column + jnp.arange(columns, dtype=jnp.int32)
    offset = row_ids[:, None] - column_ids[None, :]
    parity = (offset % 2).astype(jnp.float32)
    sign = 1.0 - 2.0 * parity
    angle = jnp.pi / order * offset.astype(jnp.float32)
    nonzero = offset != 0
    safe = jnp.where(nonzero, angle, 0.5)
    value = sign * jnp.cos(safe) / jnp.sin(safe) / order
    return jnp.where(nonzero, value, 0.0).astype(jnp.float32)

def global_columns(block_cols, send_blocks):
    rows = jnp.arange(BLOCKS, dtype=jnp.int32)
    owner = jnp.broadcast_to((rows // ROWS_DEV)[:, None], block_cols.shape).astype(jnp.int32)
    remote = block_cols - ROWS_DEV
    source = jnp.clip(remote // SLOTS, 0, N_DOM - 1).astype(jnp.int32)
    slot = jnp.clip(remote % SLOTS, 0, SLOTS - 1).astype(jnp.int32)
    far = source * ROWS_DEV + send_blocks[source, owner, slot]
    near = owner * ROWS_DEV + block_cols
    return jnp.where(block_cols < ROWS_DEV, near, far).astype(jnp.int32)

def apply_jacobian(field, conductance, capacitance, weights, columns, matrix):
    group = math.gcd(SAMPLES, 32)
    flat = columns.reshape(-1)
    blocked = field.reshape(SAMPLES // group, group, BLOCKS, BLK)

    def one_group(part):
        picked = jnp.take(part, flat, axis=1).reshape(group, BLOCKS, PER_ROW * BLK)
        return jnp.einsum('srm,rmo->sro', picked, weights, precision=lax.Precision.HIGHEST, preferred_element_type=jnp.float32)
    product = lax.map(one_group, blocked).reshape(SAMPLES, BLOCKS, 2 * BLK)
    direct = product[:, :, :BLK].reshape(SAMPLES, UNKNOWNS)
    charge = product[:, :, BLK:].reshape(SAMPLES, UNKNOWNS) + capacitance * field
    slope = jnp.dot(matrix, charge, precision=lax.Precision.HIGHEST, preferred_element_type=jnp.float32)
    return direct + conductance * field + slope

def reference(residual, conductance, capacitance, stamps, block_cols, send_blocks):
    columns = global_columns(block_cols, send_blocks)
    weights = stamps.reshape(BLOCKS, PER_ROW * BLK, 2 * BLK)
    matrix = spectral_block(0, SAMPLES, 0, SAMPLES, SAMPLES)
    scale_norm = jnp.sqrt(jnp.sum(residual * residual))
    basis_one = residual / scale_norm
    image = apply_jacobian(basis_one, conductance, capacitance, weights, columns, matrix)
    upper_one = jnp.sum(basis_one * image)
    image = image - upper_one * basis_one
    lower_one = jnp.sqrt(jnp.sum(image * image))
    basis_two = image / lower_one
    image = apply_jacobian(basis_two, conductance, capacitance, weights, columns, matrix)
    upper_two = jnp.sum(basis_one * image)
    middle_two = jnp.sum(basis_two * image)
    image = image - upper_two * basis_one - middle_two * basis_two
    lower_two = jnp.sqrt(jnp.sum(image * image))
    gram_first = upper_one * upper_one + lower_one * lower_one
    gram_cross = upper_one * upper_two + lower_one * middle_two
    gram_second = upper_two * upper_two + middle_two * middle_two + lower_two * lower_two
    target_first = scale_norm * upper_one
    target_second = scale_norm * upper_two
    determinant = gram_first * gram_second - gram_cross * gram_cross
    weight_first = (gram_second * target_first - gram_cross * target_second) / determinant
    weight_second = (gram_first * target_second - gram_cross * target_first) / determinant
    return weight_first * basis_one + weight_second * basis_two
```

```python
import jax
import jax.numpy as jnp
import ml_dtypes
import numpy as np
from jax import lax
from jax.experimental import pallas as pl
from jax.experimental.pallas import tpu as pltpu
from jax.sharding import PartitionSpec as P

MESH = pl.DeviceIdType.MESH
F32 = jnp.float32
BF16 = jnp.bfloat16

DOM = 32
SAMP = 8
ROWS = 64
SLOTS = 4
CH = 4
T = 8
N = 4096
SLAB = N // SAMP
ORDER = 256
CHUNK_ROWS = SAMP * T


def derivative_matrix():
    place = np.arange(ORDER)
    chunk, group, inner = place // CHUNK_ROWS, (place // T) % SAMP, place % T
    sample = group * (CH * T) + chunk * T + inner
    offset = sample[:, None] - sample[None, :]
    sign = 1.0 - 2.0 * (offset % 2)
    angle = np.where(offset != 0, np.pi / ORDER * offset, 0.5)
    value = np.where(offset != 0, sign / np.tan(angle) / ORDER, 0.0)
    high = value.astype(np.float32).astype(ml_dtypes.bfloat16)
    low = (value - high.astype(np.float64)).astype(np.float32).astype(ml_dtypes.bfloat16)
    return np.concatenate(
        [high.reshape(CH, CHUNK_ROWS, ORDER), low.reshape(CH, CHUNK_ROWS, ORDER)], axis=1
    )


def split(x):
    high = x.astype(BF16)
    return high, (x - high.astype(F32)).astype(BF16)


def kernel(
    cols, send, r_hbm, cond_hbm, cap_hbm, w_hbm, dm_hbm, out,
    field, cond, cap, w32, w16, dm, dup, ext,
    sbuf, rbuf, q, e, bq, be, br, bh, bl, z1b, part, red_s, red_d,
    load_sem, dom_ss, dom_rs, fq_ss, fq_rs, fe_ss, fe_rs, fr_ss, fr_rs, back_ss, back_rs,
    rs_ss, rs_rs, rd_ss, rd_rs,
):
    d = lax.axis_index("dom")
    s = lax.axis_index("samp")
    lanes = lax.broadcasted_iota(jnp.int32, (T, 128), 1)
    left = lanes < 64
    left16 = lax.broadcasted_iota(jnp.int32, (2 * T, 128), 1) < 64

    loads = [
        pltpu.make_async_copy(src, dst, load_sem.at[i])
        for i, (src, dst) in enumerate(
            ((r_hbm, field.at[0]), (cond_hbm, cond), (cap_hbm, cap), (w_hbm, w32), (dm_hbm, dm))
        )
    ]
    for copy in loads:
        copy.start()

    barrier = pltpu.get_barrier_semaphore()

    def greet_dom(k, _):
        pl.semaphore_signal(barrier, inc=1, device_id=(lax.rem(d + k, DOM), s), device_id_type=MESH)
        return 0

    def greet_samp(k, _):
        pl.semaphore_signal(barrier, inc=1, device_id=(d, lax.rem(s + k, SAMP)), device_id_type=MESH)
        return 0

    lax.fori_loop(1, DOM, greet_dom, 0)
    lax.fori_loop(1, SAMP, greet_samp, 0)

    def rows_of(c):
        return pl.ds(pl.multiple_of(c * T, T), T)

    def slab_of(k):
        return pl.ds(pl.multiple_of(k * SLAB, SLAB), SLAB)

    def place_of(c, group):
        return pl.ds(pl.multiple_of((c * SAMP + group) * T, T), T)

    def await_bytes(ref, sem):
        pltpu.make_async_copy(ref, ref, sem).wait()

    def widen(j, c):
        def step(p, _):
            tile = field[j, rows_of(c), pl.ds(pl.multiple_of(p * 128, 128), 128)]
            turned = pltpu.roll(tile, 64, 1)
            dup[2 * p] = jnp.where(left, tile, turned)
            dup[2 * p + 1] = jnp.where(left, turned, tile)
            return 0

        lax.fori_loop(0, ROWS // 2, step, 0, unroll=4)

    def pack(j, c):
        def step(k, _):
            to = lax.rem(d + k, DOM)
            for h in range(2):
                sbuf[j, c, to, h] = jnp.where(
                    left, dup[send[to * SLOTS + 2 * h]], dup[send[to * SLOTS + 2 * h + 1]]
                )
            return 0

        lax.fori_loop(1, DOM, step, 0)

    def send_dom(j, c):
        def step(k, _):
            to = lax.rem(d + k, DOM)
            pltpu.make_async_remote_copy(
                src_ref=sbuf.at[j, c, to], dst_ref=rbuf.at[j, c, d],
                send_sem=dom_ss.at[j], recv_sem=dom_rs.at[j, c],
                device_id=(to, s), device_id_type=MESH,
            ).start()
            return 0

        lax.fori_loop(1, DOM, step, 0)

    def forward(src, dst, c, send_sem, recv_sem):
        def step(k, _):
            to = lax.rem(s + k, SAMP)
            pltpu.make_async_remote_copy(
                src_ref=src.at[rows_of(c), slab_of(to)], dst_ref=dst.at[place_of(c, s)],
                send_sem=send_sem, recv_sem=recv_sem,
                device_id=(d, to), device_id_type=MESH,
            ).start()
            return 0

        lax.fori_loop(1, SAMP, step, 0)
        dst[place_of(c, s), :] = src[rows_of(c), slab_of(s)]

    def spread(tile, at):
        turned = pltpu.roll(tile, 64, 1)
        for i, both in enumerate((jnp.where(left, tile, turned), jnp.where(left, turned, tile))):
            high = both.astype(BF16).astype(F32)
            ext[at + i] = jnp.concatenate([high, both - high], axis=0).astype(BF16)

    def product(j, c):
        def local(p, _):
            spread(field[j, rows_of(c), pl.ds(pl.multiple_of(p * 128, 128), 128)], 2 * p)
            return 0

        lax.fori_loop(0, ROWS // 2, local, 0, unroll=4)
        await_bytes(rbuf.at[j, c, pl.ds(0, DOM - 1)], dom_rs.at[j, c])

        def remote(k, _):
            for h in range(2):
                spread(rbuf[j, c, k, h], ROWS + SLOTS * k + 2 * h)
            return 0

        lax.fori_loop(0, DOM, remote, 0, unroll=2)

        def one_row(row):
            picked = [ext[cols[row * 4 + k]] for k in range(4)]
            lhs = jnp.concatenate(
                [jnp.where(left16, picked[0], picked[1]), jnp.where(left16, picked[2], picked[3])], axis=1
            )
            got = jnp.dot(lhs, w16[row], preferred_element_type=F32)
            return (got[:T, :128] + (got[T:, :128] + got[:T, 128:])) + got[T:, 128:]

        def pair(p, _):
            even, odd = one_row(2 * p), one_row(2 * p + 1)
            at = pl.ds(pl.multiple_of(p * 128, 128), 128)
            value = field[j, rows_of(c), at]
            q[j, rows_of(c), at] = jnp.where(left, pltpu.roll(even, 64, 1), odd) + cap[rows_of(c), at] * value
            e[j, rows_of(c), at] = jnp.where(left, even, pltpu.roll(odd, 64, 1)) + cond[rows_of(c), at] * value
            return 0

        lax.fori_loop(0, ROWS // 2, pair, 0, unroll=4)
        forward(q.at[j], bq.at[j], c, fq_ss.at[j], fq_rs.at[j, c])
        forward(e.at[j], be.at[j], c, fe_ss.at[j], fe_rs.at[j, c])

    def split_charge(j):
        def step(c, _):
            await_bytes(bq.at[j, pl.ds(0, CHUNK_ROWS - T)], fq_rs.at[j, c])
            at = pl.ds(pl.multiple_of(c * CHUNK_ROWS, CHUNK_ROWS), CHUNK_ROWS)
            bh[at, :], bl[at, :] = split(bq[j, at, :])
            return 0

        lax.fori_loop(0, CH, step, 0)

    def slope(c):
        first = jnp.dot(dm[c], bh[...], preferred_element_type=F32)
        second = jnp.dot(dm[c, pl.ds(0, CHUNK_ROWS)], bl[...], preferred_element_type=F32)
        return first[:CHUNK_ROWS] + (first[CHUNK_ROWS:] + second)

    def fold(x):
        x = jnp.sum(x.reshape(-1, T, x.shape[-1]), axis=0)
        return sum(x[:, i * 128 : (i + 1) * 128] for i in range(x.shape[-1] // 128))

    def send_part(i):
        red_s[i, s] = part[i]

        def step(k, _):
            pltpu.make_async_remote_copy(
                src_ref=part.at[i], dst_ref=red_s.at[i, s], send_sem=rs_ss.at[i], recv_sem=rs_rs.at[i],
                device_id=(d, lax.rem(s + k, SAMP)), device_id_type=MESH,
            ).start()
            return 0

        lax.fori_loop(1, SAMP, step, 0)

    def pass_part(i):
        await_bytes(red_s.at[i, pl.ds(0, SAMP - 1)], rs_rs.at[i])
        red_d[i, d] = jnp.sum(red_s[i], axis=0)

        def step(k, _):
            pltpu.make_async_remote_copy(
                src_ref=red_d.at[i, d], dst_ref=red_d.at[i, d], send_sem=rd_ss.at[i], recv_sem=rd_rs.at[i],
                device_id=(lax.rem(d + k, DOM), s), device_id_type=MESH,
            ).start()
            return 0

        lax.fori_loop(1, DOM, step, 0)

    def sums(i):
        await_bytes(red_d.at[i, pl.ds(0, DOM - 1)], rd_rs.at[i])
        total = jnp.sum(red_d[i], axis=0)
        return [jnp.sum(total[k : k + 1, :], axis=1, keepdims=True) for k in range(3)]

    def partial_sums(parts):
        rows = [jnp.sum(x, axis=0, keepdims=True) for x in parts]
        return jnp.concatenate(rows + [jnp.zeros((T - len(rows), 128), F32)], axis=0)

    loads[0].wait()
    for j in range(2):
        for c in range(CH):
            rbuf[j, c, d] = jnp.zeros((2, T, 128), F32)
    widen(0, 0)
    pack(0, 0)
    pl.semaphore_wait(barrier, DOM + SAMP - 2)
    send_dom(0, 0)

    def early(c, _):
        widen(0, c)
        pack(0, c)
        send_dom(0, c)
        return 0

    lax.fori_loop(1, CH, early, 0)

    def share_residual(c, _):
        forward(field.at[0], br, c, fr_ss, fr_rs)
        return 0

    lax.fori_loop(0, CH, share_residual, 0)

    loads[3].wait()

    def halves(row, _):
        high, low = split(w32[row])
        w16[row, :, 0:128] = high
        w16[row, :, 128:256] = low
        return 0

    lax.fori_loop(0, ROWS, halves, 0)
    for i in (1, 2, 4):
        loads[i].wait()

    def first(c, _):
        product(0, c)
        return 0

    lax.fori_loop(0, CH, first, 0)
    split_charge(0)

    def slopes(c, _):
        at = pl.ds(pl.multiple_of(c * CHUNK_ROWS, CHUNK_ROWS), CHUNK_ROWS)
        got = slope(c)
        await_bytes(be.at[0, pl.ds(0, CHUNK_ROWS - T)], fe_rs.at[0, c])
        z1b[at, :] = got + be[0, at, :]

        def step(k, _):
            to = lax.rem(s + k, SAMP)
            pltpu.make_async_remote_copy(
                src_ref=z1b.at[place_of(c, to)], dst_ref=field.at[1, rows_of(c), slab_of(s)],
                send_sem=back_ss, recv_sem=back_rs.at[c],
                device_id=(d, to), device_id_type=MESH,
            ).start()
            return 0

        lax.fori_loop(1, SAMP, step, 0)
        field[1, rows_of(c), slab_of(s)] = z1b[place_of(c, s), :]
        return 0

    lax.fori_loop(0, CH, slopes, 0)

    def again(c, _):
        await_bytes(field.at[1, rows_of(c), pl.ds(0, N - SLAB)], back_rs.at[c])
        widen(1, c)
        pack(1, c)
        send_dom(1, c)
        return 0

    lax.fori_loop(0, CH, again, 0)

    await_bytes(br.at[pl.ds(0, ORDER - ORDER // SAMP)], fr_rs)
    part[0] = partial_sums([fold(br[...] * br[...]), fold(br[...] * z1b[...]), fold(z1b[...] * z1b[...])])
    send_part(0)
    product(1, 0)
    pass_part(0)

    def second(c, _):
        product(1, c)
        return 0

    lax.fori_loop(1, CH, second, 0)
    square, cross, image = sums(0)
    share = cross / square
    split_charge(1)

    def dots(c, carry):
        at = pl.ds(pl.multiple_of(c * CHUNK_ROWS, CHUNK_ROWS), CHUNK_ROWS)
        got = slope(c)
        await_bytes(be.at[1, pl.ds(0, CHUNK_ROWS - T)], fe_rs.at[1, c])
        one = z1b[at, :]
        two = got + be[1, at, :] - share * one
        return tuple(a + b for a, b in zip(carry, (fold(br[at, :] * two), fold(one * two), fold(two * two)), strict=True))

    zero = jnp.zeros((T, 128), F32)
    part[1] = partial_sums(lax.fori_loop(0, CH, dots, (zero, zero, zero)))
    send_part(1)
    pass_part(1)
    target, gram_cross, gram_second = sums(1)
    determinant = image * gram_second - gram_cross * gram_cross
    weight_first = (gram_second * cross - gram_cross * target) / determinant
    weight_second = (image * target - gram_cross * cross) / determinant

    def finish(c, _):
        residual = field[0, rows_of(c), :]
        out[rows_of(c), :] = weight_first * residual + weight_second * (field[1, rows_of(c), :] - share * residual)
        return 0

    lax.fori_loop(0, CH, finish, 0)

    for j in range(2):
        await_bytes(sbuf.at[j, :, pl.ds(0, DOM - 1)], dom_ss.at[j])
        await_bytes(q.at[j, :, pl.ds(0, N - SLAB)], fq_ss.at[j])
        await_bytes(e.at[j, :, pl.ds(0, N - SLAB)], fe_ss.at[j])
        await_bytes(red_s.at[j, pl.ds(0, SAMP - 1)], rs_ss.at[j])
        await_bytes(red_d.at[j, pl.ds(0, DOM - 1)], rd_ss.at[j])
    await_bytes(br.at[pl.ds(0, ORDER - ORDER // SAMP)], fr_ss)
    await_bytes(z1b.at[pl.ds(0, ORDER - ORDER // SAMP)], back_ss)


def body(residual, conductance, capacitance, stamps, block_cols, send_blocks):
    smem = pl.BlockSpec(memory_space=pltpu.SMEM)
    anywhere = pl.BlockSpec(memory_space=pl.ANY)
    dma = pltpu.SemaphoreType.DMA
    here = (CH * T, N)
    all_samples = (ORDER, SLAB)
    vmem = pltpu.VMEM
    return pl.pallas_call(
        kernel,
        out_shape=jax.ShapeDtypeStruct(here, F32),
        in_specs=[smem, smem] + [anywhere] * 5,
        out_specs=pl.BlockSpec(memory_space=pltpu.VMEM),
        scratch_shapes=[
            vmem((2, *here), F32), vmem(here, F32), vmem(here, F32),
            vmem((ROWS, 256, 128), F32), vmem((ROWS, 256, 256), BF16),
            vmem((CH, 2 * CHUNK_ROWS, ORDER), BF16),
            vmem((ROWS, T, 128), F32), vmem((ROWS + SLOTS * DOM, 2 * T, 128), BF16),
            vmem((2, CH, DOM, 2, T, 128), F32), vmem((2, CH, DOM, 2, T, 128), F32),
            vmem((2, *here), F32), vmem((2, *here), F32),
            vmem((2, *all_samples), F32), vmem((2, *all_samples), F32), vmem(all_samples, F32),
            vmem(all_samples, BF16), vmem(all_samples, BF16), vmem(all_samples, F32),
            vmem((2, T, 128), F32), vmem((2, SAMP, T, 128), F32), vmem((2, DOM, T, 128), F32),
            dma((5,)), dma((2,)), dma((2, CH)), dma((2,)), dma((2, CH)), dma((2,)), dma((2, CH)), dma, dma, dma, dma((CH,)),
            dma((2,)), dma((2,)), dma((2,)), dma((2,)),
        ],
        compiler_params=pltpu.CompilerParams(
            collective_id=0, has_side_effects=True, vmem_limit_bytes=56 * 2**20
        ),
        cost_estimate=pl.CostEstimate(flops=1_200_000_000, bytes_accessed=12_000_000, transcendentals=0),
        name="gmres_step",
    )(
        block_cols.reshape(-1), send_blocks.reshape(-1), residual, conductance, capacitance,
        stamps.reshape(ROWS, 256, 128), jnp.asarray(derivative_matrix()),
    )


def solution(mesh):
    in_specs = (
        P("samp", "dom"),
        P("samp", "dom"),
        P("samp", "dom"),
        P("dom", None, None, None),
        P("dom", None),
        P("dom", None, None),
    )
    return jax.shard_map(body, mesh=mesh, in_specs=in_specs, out_specs=P("samp", "dom"), check_vma=False)
```

```python
import jax
import jax.numpy as jnp
import ml_dtypes
import numpy as np
from jax import lax
from jax.experimental import pallas as pl
from jax.experimental.pallas import tpu as pltpu
from jax.sharding import PartitionSpec as P

MESH = pl.DeviceIdType.MESH
F32 = jnp.float32
BF16 = jnp.bfloat16

DOM = 32
SAMP = 8
ROWS = 64
SLOTS = 4
CH = 4
T = 8
N = 4096
SLAB = N // SAMP
ORDER = 256
CHUNK_ROWS = SAMP * T


def derivative_matrix():
    place = np.arange(ORDER)
    chunk, group, inner = place // CHUNK_ROWS, (place // T) % SAMP, place % T
    sample = group * (CH * T) + chunk * T + inner
    offset = sample[:, None] - sample[None, :]
    sign = 1.0 - 2.0 * (offset % 2)
    angle = np.where(offset != 0, np.pi / ORDER * offset, 0.5)
    value = np.where(offset != 0, sign / np.tan(angle) / ORDER, 0.0)
    high = value.astype(np.float32).astype(ml_dtypes.bfloat16)
    low = (value - high.astype(np.float64)).astype(np.float32).astype(ml_dtypes.bfloat16)
    return np.concatenate(
        [high.reshape(CH, CHUNK_ROWS, ORDER), low.reshape(CH, CHUNK_ROWS, ORDER)], axis=1
    )


def split(x):
    high = x.astype(BF16)
    return high, (x - high.astype(F32)).astype(BF16)


def kernel(
    cols, send, r_hbm, cond_hbm, cap_hbm, w_hbm, dm_hbm, out,
    field, cond, cap, w32, w16, dm, dup, ext,
    sbuf, rbuf, q, e, bq, be, br, bh, bl, z1b, slo, back, part, red_s, red_d,
    load_sem, dom_ss, dom_rs, fq_ss, fq_rs, fe_ss, fe_rs, fr_ss, fr_rs, back_ss, back_rs,
    rs_ss, rs_rs, rd_ss, rd_rs,
):
    d = lax.axis_index("dom")
    s = lax.axis_index("samp")
    left = lax.broadcasted_iota(jnp.int32, (T, 128), 1) < 64
    left16 = lax.broadcasted_iota(jnp.int32, (2 * T, 128), 1) < 64

    loads = [
        pltpu.make_async_copy(src, dst, load_sem.at[i])
        for i, (src, dst) in enumerate(
            ((r_hbm, field.at[0]), (w_hbm, w32), (cond_hbm, cond), (cap_hbm, cap), (dm_hbm, dm))
        )
    ]
    for copy in loads:
        copy.start()

    barrier = pltpu.get_barrier_semaphore()

    def over_dom(act):
        act(lax.rem(d + DOM // 2, DOM))

        def step(m, _):
            act(lax.rem(d + DOM // 2 + m, DOM))
            act(lax.rem(d + DOM // 2 - m, DOM))
            return 0

        lax.fori_loop(1, DOM // 2, step, 0)

    def over_samp(act):
        for k in (4, 3, 5, 2, 6, 1, 7):
            act(lax.rem(s + k, SAMP))

    def greet(to_dom, to_samp):
        pl.semaphore_signal(barrier, inc=1, device_id=(to_dom, to_samp), device_id_type=MESH)

    over_dom(lambda to: greet(to, s))
    over_samp(lambda to: greet(d, to))

    def remote(src, dst, send_sem, recv_sem, to):
        pltpu.make_async_remote_copy(
            src_ref=src, dst_ref=dst, send_sem=send_sem, recv_sem=recv_sem, device_id=to, device_id_type=MESH
        ).start()

    def rows_of(c):
        return pl.ds(pl.multiple_of(c * T, T), T)

    def chunk_of(c):
        return pl.ds(pl.multiple_of(c * CHUNK_ROWS, CHUNK_ROWS), CHUNK_ROWS)

    def tile_of(p):
        return pl.ds(pl.multiple_of(p * 128, 128), 128)

    def slab_of(k):
        return pl.ds(pl.multiple_of(k * SLAB, SLAB), SLAB)

    def place_of(c, group):
        return pl.ds(pl.multiple_of((c * SAMP + group) * T, T), T)

    def await_bytes(ref, sem):
        pltpu.make_async_copy(ref, ref, sem).wait()

    def widen(j, c):
        def step(p, _):
            tile = field[j, rows_of(c), tile_of(p)]
            turned = pltpu.roll(tile, 64, 1)
            dup[2 * p] = jnp.where(left, tile, turned)
            dup[2 * p + 1] = jnp.where(left, turned, tile)
            return 0

        lax.fori_loop(0, ROWS // 2, step, 0, unroll=16)

    def pack(j, c, to):
        for h in range(2):
            sbuf[j, c, to, h] = jnp.where(left, dup[send[2 * h, to]], dup[send[2 * h + 1, to]])

    def send_dom(j, c, to):
        remote(sbuf.at[j, c, to], rbuf.at[j, c, d], dom_ss.at[j], dom_rs.at[j, c], (to, s))

    def pack_and_send(j, c):
        def act(to):
            pack(j, c, to)
            send_dom(j, c, to)

        over_dom(act)

    def forward(src, dst, c, send_sem, recv_sem):
        over_samp(
            lambda to: remote(src.at[rows_of(c), slab_of(to)], dst.at[place_of(c, s)], send_sem, recv_sem, (d, to))
        )
        dst[place_of(c, s), :] = src[rows_of(c), slab_of(s)]

    def spread(tile, at):
        turned = pltpu.roll(tile, 64, 1)
        for i, both in enumerate((jnp.where(left, tile, turned), jnp.where(left, turned, tile))):
            high = both.astype(BF16).astype(F32)
            ext[at + i] = jnp.concatenate([high, both - high], axis=0).astype(BF16)

    def product(j, c):
        def local(p, _):
            spread(field[j, rows_of(c), tile_of(p)], 2 * p)
            return 0

        lax.fori_loop(0, ROWS // 2, local, 0, unroll=16)
        await_bytes(rbuf.at[j, c, pl.ds(0, DOM - 1)], dom_rs.at[j, c])

        def arrived(k, _):
            for h in range(2):
                spread(rbuf[j, c, k, h], ROWS + SLOTS * k + 2 * h)
            return 0

        lax.fori_loop(0, DOM, arrived, 0, unroll=8)

        def one_row(row):
            picked = [ext[cols[k, row]] for k in range(4)]
            lhs = jnp.concatenate(
                [jnp.where(left16, picked[0], picked[1]), jnp.where(left16, picked[2], picked[3])], axis=1
            )
            got = jnp.dot(lhs, w16[row], preferred_element_type=F32)
            return (got[:T, :128] + (got[T:, :128] + got[:T, 128:])) + got[T:, 128:]

        def slabs(half, _):
            for start, way in ((4, 2), (3, -2), (5, 2), (2, -2)):
                to = lax.rem(s + start + way * half, SAMP)
                for i in range(SLAB // 128):
                    p = to * (SLAB // 128) + i
                    even, odd = one_row(2 * p), one_row(2 * p + 1)
                    value = field[j, rows_of(c), tile_of(p)]
                    q[j, rows_of(c), tile_of(p)] = (
                        jnp.where(left, pltpu.roll(even, 64, 1), odd) + cap[rows_of(c), tile_of(p)] * value
                    )
                    e[j, rows_of(c), tile_of(p)] = (
                        jnp.where(left, even, pltpu.roll(odd, 64, 1)) + cond[rows_of(c), tile_of(p)] * value
                    )

                @pl.when(to != s)
                def _():
                    remote(
                        q.at[j, rows_of(c), slab_of(to)], bq.at[j, place_of(c, s)], fq_ss.at[j], fq_rs.at[j, c], (d, to)
                    )

            return 0

        lax.fori_loop(0, 2, slabs, 0)
        bq[j, place_of(c, s), :] = q[j, rows_of(c), slab_of(s)]

    def split_charge(j, c):
        await_bytes(bq.at[j, pl.ds(0, CHUNK_ROWS - T)], fq_rs.at[j, c])
        bh[chunk_of(c), :], bl[chunk_of(c), :] = split(bq[j, chunk_of(c), :])

    def slope(c):
        first = jnp.dot(dm[c], bh[...], preferred_element_type=F32)
        second = jnp.dot(dm[c, pl.ds(0, CHUNK_ROWS)], bl[...], preferred_element_type=F32)
        return first[:CHUNK_ROWS] + (first[CHUNK_ROWS:] + second)

    def fold(x):
        x = jnp.sum(x.reshape(-1, T, x.shape[-1]), axis=0)
        return sum(x[:, i * 128 : (i + 1) * 128] for i in range(x.shape[-1] // 128))

    def add_up(parts, terms):
        return tuple(a + fold(b) for a, b in zip(parts, terms, strict=True))

    def send_part(i, parts):
        rows = [jnp.sum(x, axis=0, keepdims=True) for x in parts]
        part[i] = jnp.concatenate(rows + [jnp.zeros((T - len(rows), 128), F32)], axis=0)
        over_samp(lambda to: remote(part.at[i], red_s.at[i, s], rs_ss.at[i], rs_rs.at[i], (d, to)))
        red_s[i, s] = part[i]

    def pass_part(i):
        await_bytes(red_s.at[i, pl.ds(0, SAMP - 1)], rs_rs.at[i])
        red_d[i, d] = jnp.sum(red_s[i], axis=0)
        over_dom(lambda to: remote(red_d.at[i, d], red_d.at[i, d], rd_ss.at[i], rd_rs.at[i], (to, s)))

    def sums(i):
        await_bytes(red_d.at[i, pl.ds(0, DOM - 1)], rd_rs.at[i])
        total = jnp.sum(red_d[i], axis=0)
        return [jnp.sum(total[k : k + 1, :], axis=1, keepdims=True) for k in range(3)]

    zero = jnp.zeros((T, 128), F32)

    loads[0].wait()
    for j in range(2):
        for c in range(CH):
            rbuf[j, c, d] = jnp.zeros((2, T, 128), F32)
    widen(0, 0)
    over_dom(lambda to: pack(0, 0, to))
    pl.semaphore_wait(barrier, DOM + SAMP - 2)
    over_dom(lambda to: send_dom(0, 0, to))

    def early(c, _):
        widen(0, c)
        pack_and_send(0, c)
        return 0

    lax.fori_loop(1, CH, early, 0)

    def share_residual(c, _):
        forward(field.at[0], br, c, fr_ss, fr_rs)
        return 0

    lax.fori_loop(0, CH, share_residual, 0)

    loads[1].wait()

    def halves(row, _):
        high, low = split(w32[row])
        w16[row, :, 0:128] = high
        w16[row, :, 128:256] = low
        return 0

    lax.fori_loop(0, ROWS, halves, 0)
    for i in (2, 3, 4):
        loads[i].wait()

    def first(c, _):
        product(0, c)

        @pl.when(c > 0)
        def _():
            split_charge(0, c - 1)

        return 0

    lax.fori_loop(0, CH, first, 0)
    split_charge(0, CH - 1)

    def slopes(c, _):
        slo[chunk_of(c), :] = slope(c)
        over_samp(
            lambda to: remote(
                slo.at[place_of(c, to)], back.at[rows_of(c), slab_of(s)], back_ss, back_rs.at[c], (d, to)
            )
        )
        back[rows_of(c), slab_of(s)] = slo[place_of(c, s), :]
        return 0

    lax.fori_loop(0, CH, slopes, 0)

    def again(c, _):
        await_bytes(back.at[rows_of(c), pl.ds(0, N - SLAB)], back_rs.at[c])
        field[1, rows_of(c), :] = e[0, rows_of(c), :] + back[rows_of(c), :]
        widen(1, c)
        pack_and_send(1, c)
        return 0

    lax.fori_loop(0, CH, again, 0)

    def share_direct(c, _):
        forward(e.at[0], be.at[0], c, fe_ss.at[0], fe_rs.at[0])
        return 0

    lax.fori_loop(0, CH, share_direct, 0)

    def second(c, _):
        product(1, c)
        forward(e.at[1], be.at[1], c, fe_ss.at[1], fe_rs.at[1])

        @pl.when(c == 0)
        def _():
            await_bytes(br.at[pl.ds(0, ORDER - ORDER // SAMP)], fr_rs)
            await_bytes(be.at[0, pl.ds(0, ORDER - ORDER // SAMP)], fe_rs.at[0])

            def step(i, parts):
                one = slo[chunk_of(i), :] + be[0, chunk_of(i), :]
                z1b[chunk_of(i), :] = one
                start = br[chunk_of(i), :]
                return add_up(parts, (start * start, start * one, one * one))

            send_part(0, lax.fori_loop(0, CH, step, (zero, zero, zero)))

        @pl.when(c > 0)
        def _():
            split_charge(1, c - 1)

        @pl.when(c == 1)
        def _():
            pass_part(0)

        return 0

    lax.fori_loop(0, CH, second, 0)
    square, cross, image = sums(0)
    share = cross / square
    split_charge(1, CH - 1)
    await_bytes(be.at[1, pl.ds(0, ORDER - ORDER // SAMP)], fe_rs.at[1])

    def dots(c, parts):
        one = z1b[chunk_of(c), :]
        two = slope(c) + be[1, chunk_of(c), :] - share * one
        return add_up(parts, (br[chunk_of(c), :] * two, one * two, two * two))

    send_part(1, lax.fori_loop(0, CH, dots, (zero, zero, zero)))
    pass_part(1)

    for j in range(2):
        await_bytes(sbuf.at[j, :, pl.ds(0, DOM - 1)], dom_ss.at[j])
        await_bytes(q.at[j, :, pl.ds(0, N - SLAB)], fq_ss.at[j])
        await_bytes(e.at[j, :, pl.ds(0, N - SLAB)], fe_ss.at[j])
        await_bytes(red_s.at[j, pl.ds(0, SAMP - 1)], rs_ss.at[j])
    await_bytes(br.at[pl.ds(0, ORDER - ORDER // SAMP)], fr_ss)
    await_bytes(slo.at[pl.ds(0, ORDER - ORDER // SAMP)], back_ss)

    target, gram_cross, gram_second = sums(1)
    determinant = image * gram_second - gram_cross * gram_cross
    weight_first = (gram_second * cross - gram_cross * target) / determinant
    weight_second = (image * target - gram_cross * cross) / determinant

    def finish(c, _):
        residual = field[0, rows_of(c), :]
        out[rows_of(c), :] = weight_first * residual + weight_second * (field[1, rows_of(c), :] - share * residual)
        return 0

    lax.fori_loop(0, CH, finish, 0)
    for j in range(2):
        await_bytes(red_d.at[j, pl.ds(0, DOM - 1)], rd_ss.at[j])


def body(residual, conductance, capacitance, stamps, block_cols, send_blocks):
    smem = pl.BlockSpec(memory_space=pltpu.SMEM)
    anywhere = pl.BlockSpec(memory_space=pl.ANY)
    dma = pltpu.SemaphoreType.DMA
    here = (CH * T, N)
    all_samples = (ORDER, SLAB)
    vmem = pltpu.VMEM
    return pl.pallas_call(
        kernel,
        out_shape=jax.ShapeDtypeStruct(here, F32),
        in_specs=[smem, smem] + [anywhere] * 5,
        out_specs=pl.BlockSpec(memory_space=pltpu.VMEM),
        scratch_shapes=[
            vmem((2, *here), F32), vmem(here, F32), vmem(here, F32),
            vmem((ROWS, 256, 128), F32), vmem((ROWS, 256, 256), BF16),
            vmem((CH, 2 * CHUNK_ROWS, ORDER), BF16),
            vmem((ROWS, T, 128), F32), vmem((ROWS + SLOTS * DOM, 2 * T, 128), BF16),
            vmem((2, CH, DOM, 2, T, 128), F32), vmem((2, CH, DOM, 2, T, 128), F32),
            vmem((2, *here), F32), vmem((2, *here), F32),
            vmem((2, *all_samples), F32), vmem((2, *all_samples), F32), vmem(all_samples, F32),
            vmem(all_samples, BF16), vmem(all_samples, BF16), vmem(all_samples, F32), vmem(all_samples, F32), vmem(here, F32),
            vmem((2, T, 128), F32), vmem((2, SAMP, T, 128), F32), vmem((2, DOM, T, 128), F32),
            dma((5,)), dma((2,)), dma((2, CH)), dma((2,)), dma((2, CH)), dma((2,)), dma((2,)), dma, dma, dma, dma((CH,)),
            dma((2,)), dma((2,)), dma((2,)), dma((2,)),
        ],
        compiler_params=pltpu.CompilerParams(
            collective_id=0, has_side_effects=True, vmem_limit_bytes=56 * 2**20
        ),
        cost_estimate=pl.CostEstimate(flops=1_200_000_000, bytes_accessed=12_000_000, transcendentals=0),
        name="gmres_step",
    )(
        block_cols.T, send_blocks[0].T, residual, conductance, capacitance,
        stamps.reshape(ROWS, 256, 128), jnp.asarray(derivative_matrix()),
    )


def solution(mesh):
    in_specs = (
        P("samp", "dom"),
        P("samp", "dom"),
        P("samp", "dom"),
        P("dom", None, None, None),
        P("dom", None),
        P("dom", None, None),
    )
    return jax.shard_map(body, mesh=mesh, in_specs=in_specs, out_specs=P("samp", "dom"), check_vma=False)
```

```python
import jax
import jax.numpy as jnp
import ml_dtypes
import numpy as np
from jax import lax
from jax.experimental import pallas as pl
from jax.experimental.pallas import tpu as pltpu
from jax.sharding import PartitionSpec as P

MESH = pl.DeviceIdType.MESH
F32 = jnp.float32
BF16 = jnp.bfloat16

DOM = 32
SAMP = 8
ROWS = 64
SLOTS = 4
CH = 4
T = 8
N = 4096
SLAB = N // SAMP
SQUARE = 16
ORDER = 256
CHUNK_ROWS = SAMP * T


def derivative_matrix():
    place = np.arange(ORDER)
    chunk, group, inner = place // CHUNK_ROWS, (place // T) % SAMP, place % T
    sample = group * (CH * T) + chunk * T + inner
    offset = sample[:, None] - sample[None, :]
    sign = 1.0 - 2.0 * (offset % 2)
    angle = np.where(offset != 0, np.pi / ORDER * offset, 0.5)
    value = np.where(offset != 0, sign / np.tan(angle) / ORDER, 0.0)
    high = value.astype(np.float32).astype(ml_dtypes.bfloat16)
    low = (value - high.astype(np.float64)).astype(np.float32).astype(ml_dtypes.bfloat16)
    return np.concatenate(
        [high.reshape(CH, CHUNK_ROWS, ORDER), low.reshape(CH, CHUNK_ROWS, ORDER)], axis=1
    )


def split(x):
    high = x.astype(BF16)
    return high, (x - high.astype(F32)).astype(BF16)


def kernel(
    cols_hbm, send_hbm, r_hbm, cond_hbm, cap_hbm, w_hbm, dm_hbm, out_hbm,
    cols, send, out,
    field, cond, cap, w32, w16, dm, dup, ext,
    sbuf, rbuf, q, e, bq, be, br, bh, bl, z1b, slo, back, part, red_s, red_d,
    load_sem, dom_ss, dom_rs, fq_ss, fq_rs, fe_ss, fe_rs, fr_ss, fr_rs, back_ss, back_rs,
    rs_ss, rs_rs, rd_ss, rd_rs, out_sem,
):
    d = lax.axis_index("dom")
    s = lax.axis_index("samp")
    left = lax.broadcasted_iota(jnp.int32, (T, 128), 1) < 64
    left16 = lax.broadcasted_iota(jnp.int32, (2 * T, 128), 1) < 64

    loads = [
        pltpu.make_async_copy(src, dst, load_sem.at[i])
        for i, (src, dst) in enumerate(
            ((r_hbm, field.at[0]), (send_hbm, send), (cols_hbm, cols), (w_hbm, w32), (cond_hbm, cond), (cap_hbm, cap), (dm_hbm, dm))
        )
    ]
    for copy in loads:
        copy.start()

    barrier = pltpu.get_barrier_semaphore()

    def over_dom(act):
        act(lax.rem(d + DOM // 2, DOM))

        def step(m, _):
            act(lax.rem(d + DOM // 2 + m, DOM))
            act(lax.rem(d + DOM // 2 - m, DOM))
            return 0

        lax.fori_loop(1, DOM // 2, step, 0)

    def over_samp(act):
        for k in (4, 3, 5, 2, 6, 1, 7):
            act(lax.rem(s + k, SAMP))

    z, y, x, core = lax.div(d, 4), lax.rem(d, 4), lax.div(s, 2), lax.rem(s, 2)

    def over_square(act):
        act(SQUARE // 2)

        def step(m, _):
            act(SQUARE // 2 + m)
            act(SQUARE // 2 - m)
            return 0

        lax.fori_loop(1, SQUARE // 2, step, 0)

    def in_plane(k):
        return z * 4 + lax.rem(y + lax.rem(k, 4), 4), lax.rem(s + 2 * lax.div(k, 4), SAMP)

    def in_line(k):
        return lax.rem(d + 4 * lax.div(k, 2), DOM), 2 * x + lax.rem(core + lax.rem(k, 2), 2)

    def greet(to_dom, to_samp):
        pl.semaphore_signal(barrier, inc=1, device_id=(to_dom, to_samp), device_id_type=MESH)

    over_dom(lambda to: greet(to, s))
    over_samp(lambda to: greet(d, to))

    def greet_rest(m, _):
        greet(*in_plane(4 * (1 + lax.div(m, 3)) + 1 + lax.rem(m, 3)))
        return 0

    def greet_line(m, _):
        greet(*in_line(2 * m + 1))
        return 0

    lax.fori_loop(0, 9, greet_rest, 0)
    lax.fori_loop(1, 8, greet_line, 0)

    def remote(src, dst, send_sem, recv_sem, to):
        pltpu.make_async_remote_copy(
            src_ref=src, dst_ref=dst, send_sem=send_sem, recv_sem=recv_sem, device_id=to, device_id_type=MESH
        ).start()

    def rows_of(c):
        return pl.ds(pl.multiple_of(c * T, T), T)

    def chunk_of(c):
        return pl.ds(pl.multiple_of(c * CHUNK_ROWS, CHUNK_ROWS), CHUNK_ROWS)

    def tile_of(p):
        return pl.ds(pl.multiple_of(p * 128, 128), 128)

    def slab_of(k):
        return pl.ds(pl.multiple_of(k * SLAB, SLAB), SLAB)

    def place_of(c, group):
        return pl.ds(pl.multiple_of((c * SAMP + group) * T, T), T)

    def await_bytes(ref, sem):
        pltpu.make_async_copy(ref, ref, sem).wait()

    def widen(j, c):
        def step(p, _):
            tile = field[j, rows_of(c), tile_of(p)]
            turned = pltpu.roll(tile, 64, 1)
            dup[2 * p] = jnp.where(left, tile, turned)
            dup[2 * p + 1] = jnp.where(left, turned, tile)
            return 0

        lax.fori_loop(0, ROWS // 2, step, 0, unroll=16)

    def pack(j, c, to):
        for h in range(2):
            sbuf[j, c, to, h] = jnp.where(left, dup[send[2 * h, to]], dup[send[2 * h + 1, to]])

    def send_dom(j, c, to):
        remote(sbuf.at[j, c, to], rbuf.at[j, c, d], dom_ss.at[j], dom_rs.at[j, c], (to, s))

    def pack_and_send(j, c):
        def act(to):
            pack(j, c, to)
            send_dom(j, c, to)

        over_dom(act)

    def forward(src, dst, c, send_sem, recv_sem):
        over_samp(
            lambda to: remote(src.at[rows_of(c), slab_of(to)], dst.at[place_of(c, s)], send_sem, recv_sem, (d, to))
        )
        dst[place_of(c, s), :] = src[rows_of(c), slab_of(s)]

    def spread(tile, at):
        turned = pltpu.roll(tile, 64, 1)
        for i, both in enumerate((jnp.where(left, tile, turned), jnp.where(left, turned, tile))):
            high = both.astype(BF16).astype(F32)
            ext[at + i] = jnp.concatenate([high, both - high], axis=0).astype(BF16)

    def product(j, c):
        def local(p, _):
            spread(field[j, rows_of(c), tile_of(p)], 2 * p)
            return 0

        lax.fori_loop(0, ROWS // 2, local, 0, unroll=16)
        await_bytes(rbuf.at[j, c, pl.ds(0, DOM - 1)], dom_rs.at[j, c])

        def arrived(k, _):
            for h in range(2):
                spread(rbuf[j, c, k, h], ROWS + SLOTS * k + 2 * h)
            return 0

        lax.fori_loop(0, DOM, arrived, 0, unroll=8)

        def one_row(row):
            picked = [ext[cols[k, row]] for k in range(4)]
            lhs = jnp.concatenate(
                [jnp.where(left16, picked[0], picked[1]), jnp.where(left16, picked[2], picked[3])], axis=1
            )
            got = jnp.dot(lhs, w16[row], preferred_element_type=F32)
            return (got[:T, :128] + (got[T:, :128] + got[:T, 128:])) + got[T:, 128:]

        def slabs(half, _):
            for start, way in ((4, 2), (3, -2), (5, 2), (2, -2)):
                to = lax.rem(s + start + way * half, SAMP)
                for i in range(SLAB // 128):
                    p = to * (SLAB // 128) + i
                    even, odd = one_row(2 * p), one_row(2 * p + 1)
                    value = field[j, rows_of(c), tile_of(p)]
                    q[j, rows_of(c), tile_of(p)] = (
                        jnp.where(left, pltpu.roll(even, 64, 1), odd) + cap[rows_of(c), tile_of(p)] * value
                    )
                    e[j, rows_of(c), tile_of(p)] = (
                        jnp.where(left, even, pltpu.roll(odd, 64, 1)) + cond[rows_of(c), tile_of(p)] * value
                    )

                @pl.when(to != s)
                def _():
                    remote(
                        q.at[j, rows_of(c), slab_of(to)], bq.at[j, place_of(c, s)], fq_ss.at[j], fq_rs.at[j, c], (d, to)
                    )

            return 0

        lax.fori_loop(0, 2, slabs, 0)
        bq[j, place_of(c, s), :] = q[j, rows_of(c), slab_of(s)]

    def split_charge(j, c):
        await_bytes(bq.at[j, pl.ds(0, CHUNK_ROWS - T)], fq_rs.at[j, c])
        bh[chunk_of(c), :], bl[chunk_of(c), :] = split(bq[j, chunk_of(c), :])

    def slope(c):
        first = jnp.dot(dm[c], bh[...], preferred_element_type=F32)
        second = jnp.dot(dm[c, pl.ds(0, CHUNK_ROWS)], bl[...], preferred_element_type=F32)
        return first[:CHUNK_ROWS] + (first[CHUNK_ROWS:] + second)

    def fold(x):
        x = jnp.sum(x.reshape(-1, T, x.shape[-1]), axis=0)
        return sum(x[:, i * 128 : (i + 1) * 128] for i in range(x.shape[-1] // 128))

    def add_up(parts, terms):
        return tuple(a + fold(b) for a, b in zip(parts, terms, strict=True))

    def send_part(i, parts):
        rows = [jnp.sum(x, axis=0, keepdims=True) for x in parts]
        part[i] = jnp.concatenate(rows + [jnp.zeros((T - len(rows), 128), F32)], axis=0)
        mine = x * 4 + y
        over_square(lambda k: remote(part.at[i], red_s.at[i, mine], rs_ss.at[i], rs_rs.at[i], in_plane(k)))
        red_s[i, mine] = part[i]

    def pass_part(i):
        await_bytes(red_s.at[i, pl.ds(0, SQUARE - 1)], rs_rs.at[i])
        mine = z * 2 + core
        red_d[i, mine] = jnp.sum(red_s[i], axis=0)
        over_square(lambda k: remote(red_d.at[i, mine], red_d.at[i, mine], rd_ss.at[i], rd_rs.at[i], in_line(k)))

    def sums(i):
        await_bytes(red_d.at[i, pl.ds(0, SQUARE - 1)], rd_rs.at[i])
        total = jnp.sum(red_d[i], axis=0)
        return [jnp.sum(total[k : k + 1, :], axis=1, keepdims=True) for k in range(3)]

    zero = jnp.zeros((T, 128), F32)

    loads[0].wait()
    for j in range(2):
        for c in range(CH):
            rbuf[j, c, d] = jnp.zeros((2, T, 128), F32)
    widen(0, 0)
    loads[1].wait()
    over_dom(lambda to: pack(0, 0, to))
    pl.semaphore_wait(barrier, DOM + SAMP - 2 + 9 + 7)
    over_dom(lambda to: send_dom(0, 0, to))

    def early(c, _):
        widen(0, c)
        pack_and_send(0, c)
        return 0

    lax.fori_loop(1, CH, early, 0)

    def share_residual(c, _):
        forward(field.at[0], br, c, fr_ss, fr_rs)
        return 0

    lax.fori_loop(0, CH, share_residual, 0)

    loads[3].wait()

    def halves(row, _):
        high, low = split(w32[row])
        w16[row, :, 0:128] = high
        w16[row, :, 128:256] = low
        return 0

    lax.fori_loop(0, ROWS, halves, 0)
    for i in (2, 4, 5, 6):
        loads[i].wait()

    def first(c, _):
        product(0, c)

        @pl.when(c > 0)
        def _():
            split_charge(0, c - 1)

        return 0

    lax.fori_loop(0, CH, first, 0)
    split_charge(0, CH - 1)

    def slopes(c, _):
        slo[chunk_of(c), :] = slope(c)
        over_samp(
            lambda to: remote(
                slo.at[place_of(c, to)], back.at[rows_of(c), slab_of(s)], back_ss, back_rs.at[c], (d, to)
            )
        )
        back[rows_of(c), slab_of(s)] = slo[place_of(c, s), :]
        return 0

    lax.fori_loop(0, CH, slopes, 0)

    def again(c, _):
        await_bytes(back.at[rows_of(c), pl.ds(0, N - SLAB)], back_rs.at[c])
        field[1, rows_of(c), :] = e[0, rows_of(c), :] + back[rows_of(c), :]
        widen(1, c)
        pack_and_send(1, c)
        return 0

    lax.fori_loop(0, CH, again, 0)

    def share_direct(c, _):
        forward(e.at[0], be.at[0], c, fe_ss.at[0], fe_rs.at[0])
        return 0

    lax.fori_loop(0, CH, share_direct, 0)

    def second(c, _):
        product(1, c)
        forward(e.at[1], be.at[1], c, fe_ss.at[1], fe_rs.at[1])

        @pl.when(c == 0)
        def _():
            await_bytes(br.at[pl.ds(0, ORDER - ORDER // SAMP)], fr_rs)
            await_bytes(be.at[0, pl.ds(0, ORDER - ORDER // SAMP)], fe_rs.at[0])

            def step(i, parts):
                one = slo[chunk_of(i), :] + be[0, chunk_of(i), :]
                z1b[chunk_of(i), :] = one
                start = br[chunk_of(i), :]
                return add_up(parts, (start * start, start * one, one * one))

            send_part(0, lax.fori_loop(0, CH, step, (zero, zero, zero)))

        @pl.when(c > 0)
        def _():
            split_charge(1, c - 1)

        @pl.when(c == 1)
        def _():
            pass_part(0)

        return 0

    lax.fori_loop(0, CH, second, 0)
    square, cross, image = sums(0)
    share = cross / square
    split_charge(1, CH - 1)

    def last_slopes(c, _):
        bq[0, chunk_of(c), :] = slope(c)
        return 0

    lax.fori_loop(0, CH, last_slopes, 0)
    await_bytes(be.at[1, pl.ds(0, ORDER - ORDER // SAMP)], fe_rs.at[1])

    def dots(c, parts):
        one = z1b[chunk_of(c), :]
        two = bq[0, chunk_of(c), :] + be[1, chunk_of(c), :] - share * one
        return add_up(parts, (br[chunk_of(c), :] * two, one * two, two * two))

    send_part(1, lax.fori_loop(0, CH, dots, (zero, zero, zero)))
    pass_part(1)

    for j in range(2):
        await_bytes(sbuf.at[j, :, pl.ds(0, DOM - 1)], dom_ss.at[j])
        await_bytes(q.at[j, :, pl.ds(0, N - SLAB)], fq_ss.at[j])
        await_bytes(e.at[j, :, pl.ds(0, N - SLAB)], fe_ss.at[j])
        await_bytes(red_s.at[j, pl.ds(0, SQUARE - 1)], rs_ss.at[j])
    await_bytes(br.at[pl.ds(0, ORDER - ORDER // SAMP)], fr_ss)
    await_bytes(slo.at[pl.ds(0, ORDER - ORDER // SAMP)], back_ss)

    target, gram_cross, gram_second = sums(1)
    determinant = image * gram_second - gram_cross * gram_cross
    weight_first = (gram_second * cross - gram_cross * target) / determinant
    weight_second = (image * target - gram_cross * cross) / determinant

    def finish(c, _):
        residual = field[0, rows_of(c), :]
        out[rows_of(c), :] = weight_first * residual + weight_second * (field[1, rows_of(c), :] - share * residual)
        pltpu.make_async_copy(out.at[rows_of(c)], out_hbm.at[rows_of(c)], out_sem).start()
        return 0

    lax.fori_loop(0, CH, finish, 0)
    for j in range(2):
        await_bytes(red_d.at[j, pl.ds(0, SQUARE - 1)], rd_ss.at[j])
    pltpu.make_async_copy(out, out_hbm, out_sem).wait()


def body(residual, conductance, capacitance, stamps, block_cols, send_blocks):
    anywhere = pl.BlockSpec(memory_space=pl.ANY)
    dma = pltpu.SemaphoreType.DMA
    here = (CH * T, N)
    all_samples = (ORDER, SLAB)
    vmem = pltpu.VMEM
    return pl.pallas_call(
        kernel,
        out_shape=jax.ShapeDtypeStruct(here, F32),
        in_specs=[anywhere] * 7,
        out_specs=anywhere,
        scratch_shapes=[
            pltpu.SMEM((4, ROWS), jnp.int32), pltpu.SMEM((SLOTS, DOM), jnp.int32), vmem(here, F32),
            vmem((2, *here), F32), vmem(here, F32), vmem(here, F32),
            vmem((ROWS, 256, 128), F32), vmem((ROWS, 256, 256), BF16),
            vmem((CH, 2 * CHUNK_ROWS, ORDER), BF16),
            vmem((ROWS, T, 128), F32), vmem((ROWS + SLOTS * DOM, 2 * T, 128), BF16),
            vmem((2, CH, DOM, 2, T, 128), F32), vmem((2, CH, DOM, 2, T, 128), F32),
            vmem((2, *here), F32), vmem((2, *here), F32),
            vmem((2, *all_samples), F32), vmem((2, *all_samples), F32), vmem(all_samples, F32),
            vmem(all_samples, BF16), vmem(all_samples, BF16), vmem(all_samples, F32), vmem(all_samples, F32), vmem(here, F32),
            vmem((2, T, 128), F32), vmem((2, SQUARE, T, 128), F32), vmem((2, SQUARE, T, 128), F32),
            dma((7,)), dma((2,)), dma((2, CH)), dma((2,)), dma((2, CH)), dma((2,)), dma((2,)), dma, dma, dma, dma((CH,)),
            dma((2,)), dma((2,)), dma((2,)), dma((2,)), dma,
        ],
        compiler_params=pltpu.CompilerParams(
            collective_id=0, has_side_effects=True, vmem_limit_bytes=56 * 2**20
        ),
        cost_estimate=pl.CostEstimate(flops=1_200_000_000, bytes_accessed=12_000_000, transcendentals=0),
        name="gmres_step",
    )(
        block_cols.T, send_blocks[0].T, residual, conductance, capacitance,
        stamps.reshape(ROWS, 256, 128), jnp.asarray(derivative_matrix()),
    )


def solution(mesh):
    in_specs = (
        P("samp", "dom"),
        P("samp", "dom"),
        P("samp", "dom"),
        P("dom", None, None, None),
        P("dom", None),
        P("dom", None, None),
    )
    return jax.shard_map(body, mesh=mesh, in_specs=in_specs, out_specs=P("samp", "dom"), check_vma=False)
```

```python
import jax
import jax.numpy as jnp
import ml_dtypes
import numpy as np
from jax import lax
from jax.experimental import pallas as pl
from jax.experimental.pallas import tpu as pltpu
from jax.sharding import PartitionSpec as P

MESH = pl.DeviceIdType.MESH
F32 = jnp.float32
BF16 = jnp.bfloat16

DOM = 32
SAMP = 8
ROWS = 64
SLOTS = 4
CH = 4
T = 8
N = 4096
SLAB = N // SAMP
SQUARE = 16
ORDER = 256
CHUNK_ROWS = SAMP * T


def derivative_matrix():
    place = np.arange(ORDER)
    chunk, group, inner = place // CHUNK_ROWS, (place // T) % SAMP, place % T
    sample = group * (CH * T) + chunk * T + inner
    offset = sample[:, None] - sample[None, :]
    sign = 1.0 - 2.0 * (offset % 2)
    angle = np.where(offset != 0, np.pi / ORDER * offset, 0.5)
    value = np.where(offset != 0, sign / np.tan(angle) / ORDER, 0.0)
    high = value.astype(np.float32).astype(ml_dtypes.bfloat16)
    low = (value - high.astype(np.float64)).astype(np.float32).astype(ml_dtypes.bfloat16)
    return np.concatenate(
        [high.reshape(CH, CHUNK_ROWS, ORDER), low.reshape(CH, CHUNK_ROWS, ORDER)], axis=1
    )


def split(x):
    high = x.astype(BF16)
    return high, (x - high.astype(F32)).astype(BF16)


def kernel(
    cols_hbm, send_hbm, r_hbm, cond_hbm, cap_hbm, w_hbm, dm_hbm, out_hbm,
    cols, send, out,
    field, cond, cap, w32, w16, dm, dup, ext,
    sbuf, rbuf, q, e, bq, be, br, bh, bl, z1b, slo, back, part, red_s, red_d,
    load_sem, dom_ss, dom_rs, fq_ss, fq_rs, fe_ss, fe_rs, fr_ss, fr_rs, back_ss, back_rs,
    rs_ss, rs_rs, rd_ss, rd_rs, out_sem,
):
    d = lax.axis_index("dom")
    s = lax.axis_index("samp")
    left = lax.broadcasted_iota(jnp.int32, (T, 128), 1) < 64
    left16 = lax.broadcasted_iota(jnp.int32, (2 * T, 128), 1) < 64

    loads = [
        pltpu.make_async_copy(src, dst, load_sem.at[i])
        for i, (src, dst) in enumerate(
            ((r_hbm, field.at[0]), (send_hbm, send), (cols_hbm, cols), (w_hbm, w32), (cond_hbm, cond), (cap_hbm, cap), (dm_hbm, dm))
        )
    ]
    for copy in loads:
        copy.start()

    barrier = pltpu.get_barrier_semaphore()

    def over_dom(act):
        act(lax.rem(d + DOM // 2, DOM))

        def step(m, _):
            act(lax.rem(d + DOM // 2 + m, DOM))
            act(lax.rem(d + DOM // 2 - m, DOM))
            return 0

        lax.fori_loop(1, DOM // 2, step, 0, unroll=3)

    def over_samp(act):
        for k in (4, 3, 5, 2, 6, 1, 7):
            act(lax.rem(s + k, SAMP))

    z, y, x, core = lax.div(d, 4), lax.rem(d, 4), lax.div(s, 2), lax.rem(s, 2)

    def over_square(act):
        act(SQUARE // 2)

        def step(m, _):
            act(SQUARE // 2 + m)
            act(SQUARE // 2 - m)
            return 0

        lax.fori_loop(1, SQUARE // 2, step, 0)

    def in_plane(k):
        return z * 4 + lax.rem(y + lax.rem(k, 4), 4), lax.rem(s + 2 * lax.div(k, 4), SAMP)

    def in_line(k):
        return lax.rem(d + 4 * lax.div(k, 2), DOM), 2 * x + lax.rem(core + lax.rem(k, 2), 2)

    def greet(to_dom, to_samp):
        pl.semaphore_signal(barrier, inc=1, device_id=(to_dom, to_samp), device_id_type=MESH)

    over_dom(lambda to: greet(to, s))
    over_samp(lambda to: greet(d, to))

    def greet_rest(m, _):
        greet(*in_plane(4 * (1 + lax.div(m, 3)) + 1 + lax.rem(m, 3)))
        return 0

    def greet_line(m, _):
        greet(*in_line(2 * m + 1))
        return 0

    lax.fori_loop(0, 9, greet_rest, 0)
    lax.fori_loop(1, 8, greet_line, 0)

    def remote(src, dst, send_sem, recv_sem, to):
        pltpu.make_async_remote_copy(
            src_ref=src, dst_ref=dst, send_sem=send_sem, recv_sem=recv_sem, device_id=to, device_id_type=MESH
        ).start()

    def rows_of(c):
        return pl.ds(pl.multiple_of(c * T, T), T)

    def chunk_of(c):
        return pl.ds(pl.multiple_of(c * CHUNK_ROWS, CHUNK_ROWS), CHUNK_ROWS)

    def tile_of(p):
        return pl.ds(pl.multiple_of(p * 128, 128), 128)

    def slab_of(k):
        return pl.ds(pl.multiple_of(k * SLAB, SLAB), SLAB)

    def place_of(c, group):
        return pl.ds(pl.multiple_of((c * SAMP + group) * T, T), T)

    def await_bytes(ref, sem):
        pltpu.make_async_copy(ref, ref, sem).wait()

    def widen(j, c):
        def step(p, _):
            tile = field[j, rows_of(c), tile_of(p)]
            turned = pltpu.roll(tile, 64, 1)
            dup[2 * p] = jnp.where(left, tile, turned)
            dup[2 * p + 1] = jnp.where(left, turned, tile)
            return 0

        lax.fori_loop(0, ROWS // 2, step, 0, unroll=16)

    def pack(j, c, to):
        for h in range(2):
            sbuf[j, c, to, h] = jnp.where(left, dup[send[2 * h, to]], dup[send[2 * h + 1, to]])

    def send_dom(j, c, to):
        remote(sbuf.at[j, c, to], rbuf.at[j, c, d], dom_ss.at[j], dom_rs.at[j, c], (to, s))

    def pack_and_send(j, c):
        def act(to):
            pack(j, c, to)
            send_dom(j, c, to)

        over_dom(act)

    def forward(src, dst, c, send_sem, recv_sem):
        over_samp(
            lambda to: remote(src.at[rows_of(c), slab_of(to)], dst.at[place_of(c, s)], send_sem, recv_sem, (d, to))
        )
        dst[place_of(c, s), :] = src[rows_of(c), slab_of(s)]

    def spread(tile, at):
        turned = pltpu.roll(tile, 64, 1)
        for i, both in enumerate((jnp.where(left, tile, turned), jnp.where(left, turned, tile))):
            high = both.astype(BF16).astype(F32)
            ext[at + i] = jnp.concatenate([high, both - high], axis=0).astype(BF16)

    def product(j, c):
        def local(p, _):
            spread(field[j, rows_of(c), tile_of(p)], 2 * p)
            return 0

        lax.fori_loop(0, ROWS // 2, local, 0, unroll=32)
        await_bytes(rbuf.at[j, c, pl.ds(0, DOM - 1)], dom_rs.at[j, c])

        def arrived(k, _):
            for h in range(2):
                spread(rbuf[j, c, k, h], ROWS + SLOTS * k + 2 * h)
            return 0

        lax.fori_loop(0, DOM, arrived, 0, unroll=16)

        def one_row(row):
            picked = [ext[cols[k, row]] for k in range(4)]
            lhs = jnp.concatenate(
                [jnp.where(left16, picked[0], picked[1]), jnp.where(left16, picked[2], picked[3])], axis=1
            )
            got = jnp.dot(lhs, w16[row], preferred_element_type=F32)
            return (got[:T, :128] + (got[T:, :128] + got[:T, 128:])) + got[T:, 128:]

        def slabs(half, _):
            for start, way in ((4, 2), (3, -2), (5, 2), (2, -2)):
                to = lax.rem(s + start + way * half, SAMP)
                for i in range(SLAB // 128):
                    p = to * (SLAB // 128) + i
                    even, odd = one_row(2 * p), one_row(2 * p + 1)
                    value = field[j, rows_of(c), tile_of(p)]
                    q[j, rows_of(c), tile_of(p)] = (
                        jnp.where(left, pltpu.roll(even, 64, 1), odd) + cap[rows_of(c), tile_of(p)] * value
                    )
                    e[j, rows_of(c), tile_of(p)] = (
                        jnp.where(left, even, pltpu.roll(odd, 64, 1)) + cond[rows_of(c), tile_of(p)] * value
                    )

                @pl.when(to != s)
                def _():
                    remote(
                        q.at[j, rows_of(c), slab_of(to)], bq.at[j, place_of(c, s)], fq_ss.at[j], fq_rs.at[j, c], (d, to)
                    )

            return 0

        lax.fori_loop(0, 2, slabs, 0)
        bq[j, place_of(c, s), :] = q[j, rows_of(c), slab_of(s)]

    def split_charge(j, c):
        await_bytes(bq.at[j, pl.ds(0, CHUNK_ROWS - T)], fq_rs.at[j, c])
        bh[chunk_of(c), :], bl[chunk_of(c), :] = split(bq[j, chunk_of(c), :])

    def slope(c):
        first = jnp.dot(dm[c], bh[...], preferred_element_type=F32)
        second = jnp.dot(dm[c, pl.ds(0, CHUNK_ROWS)], bl[...], preferred_element_type=F32)
        return first[:CHUNK_ROWS] + (first[CHUNK_ROWS:] + second)

    def fold(x):
        x = jnp.sum(x.reshape(-1, T, x.shape[-1]), axis=0)
        return sum(x[:, i * 128 : (i + 1) * 128] for i in range(x.shape[-1] // 128))

    def add_up(parts, terms):
        return tuple(a + fold(b) for a, b in zip(parts, terms, strict=True))

    def send_part(i, parts):
        rows = [jnp.sum(x, axis=0, keepdims=True) for x in parts]
        part[i] = jnp.concatenate(rows + [jnp.zeros((T - len(rows), 128), F32)], axis=0)
        mine = x * 4 + y
        over_square(lambda k: remote(part.at[i], red_s.at[i, mine], rs_ss.at[i], rs_rs.at[i], in_plane(k)))
        red_s[i, mine] = part[i]

    def pass_part(i):
        await_bytes(red_s.at[i, pl.ds(0, SQUARE - 1)], rs_rs.at[i])
        mine = z * 2 + core
        red_d[i, mine] = jnp.sum(red_s[i], axis=0)
        over_square(lambda k: remote(red_d.at[i, mine], red_d.at[i, mine], rd_ss.at[i], rd_rs.at[i], in_line(k)))

    def sums(i):
        await_bytes(red_d.at[i, pl.ds(0, SQUARE - 1)], rd_rs.at[i])
        total = jnp.sum(red_d[i], axis=0)
        return [jnp.sum(total[k : k + 1, :], axis=1, keepdims=True) for k in range(3)]

    zero = jnp.zeros((T, 128), F32)

    loads[0].wait()
    for j in range(2):
        for c in range(CH):
            rbuf[j, c, d] = jnp.zeros((2, T, 128), F32)
    widen(0, 0)
    loads[1].wait()
    over_dom(lambda to: pack(0, 0, to))
    pl.semaphore_wait(barrier, DOM + SAMP - 2 + 9 + 7)
    over_dom(lambda to: send_dom(0, 0, to))

    def early(c, _):
        widen(0, c)
        pack_and_send(0, c)
        return 0

    lax.fori_loop(1, CH, early, 0)

    def share_residual(c, _):
        forward(field.at[0], br, c, fr_ss, fr_rs)
        return 0

    lax.fori_loop(0, CH, share_residual, 0)

    loads[3].wait()

    def halves(row, _):
        high, low = split(w32[row])
        w16[row, :, 0:128] = high
        w16[row, :, 128:256] = low
        return 0

    lax.fori_loop(0, ROWS, halves, 0, unroll=2)
    for i in (2, 4, 5, 6):
        loads[i].wait()

    def first(c, _):
        product(0, c)

        @pl.when(c > 0)
        def _():
            split_charge(0, c - 1)

        return 0

    lax.fori_loop(0, CH, first, 0)
    split_charge(0, CH - 1)

    def slopes(c, _):
        slo[chunk_of(c), :] = slope(c)
        over_samp(
            lambda to: remote(
                slo.at[place_of(c, to)], back.at[rows_of(c), slab_of(s)], back_ss, back_rs.at[c], (d, to)
            )
        )
        back[rows_of(c), slab_of(s)] = slo[place_of(c, s), :]
        return 0

    lax.fori_loop(0, CH, slopes, 0)

    def again(c, _):
        await_bytes(back.at[rows_of(c), pl.ds(0, N - SLAB)], back_rs.at[c])
        field[1, rows_of(c), :] = e[0, rows_of(c), :] + back[rows_of(c), :]
        widen(1, c)
        pack_and_send(1, c)
        return 0

    lax.fori_loop(0, CH, again, 0)

    def share_direct(c, _):
        forward(e.at[0], be.at[0], c, fe_ss.at[0], fe_rs.at[0])
        return 0

    lax.fori_loop(0, CH, share_direct, 0)

    def second(c, _):
        product(1, c)
        forward(e.at[1], be.at[1], c, fe_ss.at[1], fe_rs.at[1])

        @pl.when(c == 0)
        def _():
            await_bytes(br.at[pl.ds(0, ORDER - ORDER // SAMP)], fr_rs)
            await_bytes(be.at[0, pl.ds(0, ORDER - ORDER // SAMP)], fe_rs.at[0])

            def step(i, parts):
                one = slo[chunk_of(i), :] + be[0, chunk_of(i), :]
                z1b[chunk_of(i), :] = one
                start = br[chunk_of(i), :]
                return add_up(parts, (start * start, start * one, one * one))

            send_part(0, lax.fori_loop(0, CH, step, (zero, zero, zero)))

        @pl.when(c > 0)
        def _():
            split_charge(1, c - 1)

        @pl.when(c == 1)
        def _():
            pass_part(0)

        return 0

    lax.fori_loop(0, CH, second, 0)
    square, cross, image = sums(0)
    share = cross / square
    split_charge(1, CH - 1)

    def last_slopes(c, _):
        bq[0, chunk_of(c), :] = slope(c)
        return 0

    lax.fori_loop(0, CH, last_slopes, 0, unroll=4)
    await_bytes(be.at[1, pl.ds(0, ORDER - ORDER // SAMP)], fe_rs.at[1])

    def dots(c, parts):
        one = z1b[chunk_of(c), :]
        two = bq[0, chunk_of(c), :] + be[1, chunk_of(c), :] - share * one
        return add_up(parts, (br[chunk_of(c), :] * two, one * two, two * two))

    send_part(1, lax.fori_loop(0, CH, dots, (zero, zero, zero), unroll=4))
    pass_part(1)

    for j in range(2):
        await_bytes(sbuf.at[j, :, pl.ds(0, DOM - 1)], dom_ss.at[j])
        await_bytes(q.at[j, :, pl.ds(0, N - SLAB)], fq_ss.at[j])
        await_bytes(e.at[j, :, pl.ds(0, N - SLAB)], fe_ss.at[j])
        await_bytes(red_s.at[j, pl.ds(0, SQUARE - 1)], rs_ss.at[j])
    await_bytes(br.at[pl.ds(0, ORDER - ORDER // SAMP)], fr_ss)
    await_bytes(slo.at[pl.ds(0, ORDER - ORDER // SAMP)], back_ss)

    target, gram_cross, gram_second = sums(1)
    determinant = image * gram_second - gram_cross * gram_cross
    weight_first = (gram_second * cross - gram_cross * target) / determinant
    weight_second = (image * target - gram_cross * cross) / determinant

    def finish(c, _):
        residual = field[0, rows_of(c), :]
        out[rows_of(c), :] = weight_first * residual + weight_second * (field[1, rows_of(c), :] - share * residual)
        pltpu.make_async_copy(out.at[rows_of(c)], out_hbm.at[rows_of(c)], out_sem).start()
        return 0

    lax.fori_loop(0, CH, finish, 0)
    for j in range(2):
        await_bytes(red_d.at[j, pl.ds(0, SQUARE - 1)], rd_ss.at[j])
    pltpu.make_async_copy(out, out_hbm, out_sem).wait()


def body(residual, conductance, capacitance, stamps, block_cols, send_blocks):
    anywhere = pl.BlockSpec(memory_space=pl.ANY)
    dma = pltpu.SemaphoreType.DMA
    here = (CH * T, N)
    all_samples = (ORDER, SLAB)
    vmem = pltpu.VMEM
    return pl.pallas_call(
        kernel,
        out_shape=jax.ShapeDtypeStruct(here, F32),
        in_specs=[anywhere] * 7,
        out_specs=anywhere,
        scratch_shapes=[
            pltpu.SMEM((4, ROWS), jnp.int32), pltpu.SMEM((SLOTS, DOM), jnp.int32), vmem(here, F32),
            vmem((2, *here), F32), vmem(here, F32), vmem(here, F32),
            vmem((ROWS, 256, 128), F32), vmem((ROWS, 256, 256), BF16),
            vmem((CH, 2 * CHUNK_ROWS, ORDER), BF16),
            vmem((ROWS, T, 128), F32), vmem((ROWS + SLOTS * DOM, 2 * T, 128), BF16),
            vmem((2, CH, DOM, 2, T, 128), F32), vmem((2, CH, DOM, 2, T, 128), F32),
            vmem((2, *here), F32), vmem((2, *here), F32),
            vmem((2, *all_samples), F32), vmem((2, *all_samples), F32), vmem(all_samples, F32),
            vmem(all_samples, BF16), vmem(all_samples, BF16), vmem(all_samples, F32), vmem(all_samples, F32), vmem(here, F32),
            vmem((2, T, 128), F32), vmem((2, SQUARE, T, 128), F32), vmem((2, SQUARE, T, 128), F32),
            dma((7,)), dma((2,)), dma((2, CH)), dma((2,)), dma((2, CH)), dma((2,)), dma((2,)), dma, dma, dma, dma((CH,)),
            dma((2,)), dma((2,)), dma((2,)), dma((2,)), dma,
        ],
        compiler_params=pltpu.CompilerParams(
            collective_id=0, has_side_effects=True, vmem_limit_bytes=56 * 2**20
        ),
        cost_estimate=pl.CostEstimate(flops=1_200_000_000, bytes_accessed=12_000_000, transcendentals=0),
        name="gmres_step",
    )(
        block_cols.T, send_blocks[0].T, residual, conductance, capacitance,
        stamps.reshape(ROWS, 256, 128), jnp.asarray(derivative_matrix()),
    )


def solution(mesh):
    in_specs = (
        P("samp", "dom"),
        P("samp", "dom"),
        P("samp", "dom"),
        P("dom", None, None, None),
        P("dom", None),
        P("dom", None, None),
    )
    return jax.shard_map(body, mesh=mesh, in_specs=in_specs, out_specs=P("samp", "dom"), check_vma=False)
```

```python
import jax
import jax.numpy as jnp
import ml_dtypes
import numpy as np
from jax import lax
from jax.experimental import pallas as pl
from jax.experimental.pallas import tpu as pltpu
from jax.sharding import PartitionSpec as P

MESH = pl.DeviceIdType.MESH
F32 = jnp.float32
BF16 = jnp.bfloat16

DOM = 32
SAMP = 8
ROWS = 64
SLOTS = 4
CH = 4
T = 8
N = 4096
SLAB = N // SAMP
SQUARE = 16
ORDER = 256
CHUNK_ROWS = SAMP * T


def derivative_matrix():
    place = np.arange(ORDER)
    chunk, group, inner = place // CHUNK_ROWS, (place // T) % SAMP, place % T
    sample = group * (CH * T) + chunk * T + inner
    offset = sample[:, None] - sample[None, :]
    sign = 1.0 - 2.0 * (offset % 2)
    angle = np.where(offset != 0, np.pi / ORDER * offset, 0.5)
    value = np.where(offset != 0, sign / np.tan(angle) / ORDER, 0.0)
    high = value.astype(np.float32).astype(ml_dtypes.bfloat16)
    low = (value - high.astype(np.float64)).astype(np.float32).astype(ml_dtypes.bfloat16)
    return np.concatenate(
        [high.reshape(CH, CHUNK_ROWS, ORDER), low.reshape(CH, CHUNK_ROWS, ORDER)], axis=1
    )


def split(x):
    high = x.astype(BF16)
    return high, (x - high.astype(F32)).astype(BF16)


def kernel(
    cols_hbm, send_hbm, r_hbm, cond_hbm, cap_hbm, w_hbm, dm_hbm, out_hbm,
    cols, send, out,
    field, cond, cap, w32, w16, dm, dup, ext,
    sbuf, rbuf, q, e, bq, be, br, bh, bl, z1b, slo, back, part, red_s, red_d,
    load_sem, dom_ss, dom_rs, fq_ss, fq_rs, fe_ss, fe_rs, fr_ss, fr_rs, back_ss, back_rs,
    rs_ss, rs_rs, rd_ss, rd_rs, out_sem,
):
    d = lax.axis_index("dom")
    s = lax.axis_index("samp")
    left = lax.broadcasted_iota(jnp.int32, (T, 128), 1) < 64
    left16 = lax.broadcasted_iota(jnp.int32, (2 * T, 128), 1) < 64

    loads = [
        pltpu.make_async_copy(src, dst, load_sem.at[i])
        for i, (src, dst) in enumerate(
            ((r_hbm, field.at[0]), (send_hbm, send), (cols_hbm, cols), (w_hbm, w32), (cond_hbm, cond), (cap_hbm, cap), (dm_hbm, dm))
        )
    ]
    for copy in loads:
        copy.start()

    barrier = pltpu.get_barrier_semaphore()

    def over_dom(act):
        act(lax.rem(d + DOM // 2, DOM))

        def step(m, _):
            act(lax.rem(d + DOM // 2 + m, DOM))
            act(lax.rem(d + DOM // 2 - m, DOM))
            return 0

        lax.fori_loop(1, DOM // 2, step, 0, unroll=3)

    def over_samp(act):
        for k in (4, 3, 5, 2, 6, 1, 7):
            act(lax.rem(s + k, SAMP))

    z, y, x, core = lax.div(d, 4), lax.rem(d, 4), lax.div(s, 2), lax.rem(s, 2)

    def over_square(act):
        act(SQUARE // 2)

        def step(m, _):
            act(SQUARE // 2 + m)
            act(SQUARE // 2 - m)
            return 0

        lax.fori_loop(1, SQUARE // 2, step, 0)

    def in_plane(k):
        return z * 4 + lax.rem(y + lax.rem(k, 4), 4), lax.rem(s + 2 * lax.div(k, 4), SAMP)

    def in_line(k):
        return lax.rem(d + 4 * lax.div(k, 2), DOM), 2 * x + lax.rem(core + lax.rem(k, 2), 2)

    def greet(to_dom, to_samp):
        pl.semaphore_signal(barrier, inc=1, device_id=(to_dom, to_samp), device_id_type=MESH)

    over_dom(lambda to: greet(to, s))
    over_samp(lambda to: greet(d, to))

    def greet_rest(m, _):
        greet(*in_plane(4 * (1 + lax.div(m, 3)) + 1 + lax.rem(m, 3)))
        return 0

    def greet_line(m, _):
        greet(*in_line(2 * m + 1))
        return 0

    lax.fori_loop(0, 9, greet_rest, 0)
    lax.fori_loop(1, 8, greet_line, 0)

    def remote(src, dst, send_sem, recv_sem, to):
        pltpu.make_async_remote_copy(
            src_ref=src, dst_ref=dst, send_sem=send_sem, recv_sem=recv_sem, device_id=to, device_id_type=MESH
        ).start()

    def rows_of(c):
        return pl.ds(pl.multiple_of(c * T, T), T)

    def chunk_of(c):
        return pl.ds(pl.multiple_of(c * CHUNK_ROWS, CHUNK_ROWS), CHUNK_ROWS)

    def tile_of(p):
        return pl.ds(pl.multiple_of(p * 128, 128), 128)

    def slab_of(k):
        return pl.ds(pl.multiple_of(k * SLAB, SLAB), SLAB)

    def place_of(c, group):
        return pl.ds(pl.multiple_of((c * SAMP + group) * T, T), T)

    def await_bytes(ref, sem):
        pltpu.make_async_copy(ref, ref, sem).wait()

    def widen(j, c):
        def step(p, _):
            tile = field[j, rows_of(c), tile_of(p)]
            turned = pltpu.roll(tile, 64, 1)
            dup[2 * p] = jnp.where(left, tile, turned)
            dup[2 * p + 1] = jnp.where(left, turned, tile)
            return 0

        lax.fori_loop(0, ROWS // 2, step, 0, unroll=16)

    def pack(j, c, to):
        for h in range(2):
            sbuf[j, c, to, h] = jnp.where(left, dup[send[2 * h, to]], dup[send[2 * h + 1, to]])

    def send_dom(j, c, to):
        remote(sbuf.at[j, c, to], rbuf.at[j, c, d], dom_ss.at[j], dom_rs.at[j, c], (to, s))

    def pack_and_send(j, c):
        def act(to):
            pack(j, c, to)
            send_dom(j, c, to)

        over_dom(act)

    def forward(src, dst, c, send_sem, recv_sem):
        over_samp(
            lambda to: remote(src.at[rows_of(c), slab_of(to)], dst.at[place_of(c, s)], send_sem, recv_sem, (d, to))
        )
        dst[place_of(c, s), :] = src[rows_of(c), slab_of(s)]

    def spread(tile, at):
        turned = pltpu.roll(tile, 64, 1)
        for i, both in enumerate((jnp.where(left, tile, turned), jnp.where(left, turned, tile))):
            high = both.astype(BF16).astype(F32)
            ext[at + i] = jnp.concatenate([high, both - high], axis=0).astype(BF16)

    def product(j, c):
        def local(p, _):
            spread(field[j, rows_of(c), tile_of(p)], 2 * p)
            return 0

        lax.fori_loop(0, ROWS // 2, local, 0, unroll=32)
        await_bytes(rbuf.at[j, c, pl.ds(0, DOM - 1)], dom_rs.at[j, c])

        def arrived(k, _):
            for h in range(2):
                spread(rbuf[j, c, k, h], ROWS + SLOTS * k + 2 * h)
            return 0

        lax.fori_loop(0, DOM, arrived, 0, unroll=16)

        def one_row(row):
            picked = [ext[cols[k, row]] for k in range(4)]
            lhs = jnp.concatenate(
                [jnp.where(left16, picked[0], picked[1]), jnp.where(left16, picked[2], picked[3])], axis=1
            )
            got = jnp.dot(lhs, w16[row], preferred_element_type=F32)
            return (got[:T, :128] + (got[T:, :128] + got[:T, 128:])) + got[T:, 128:]

        def slabs(half, _):
            for start, way in ((4, 2), (3, -2), (5, 2), (2, -2)):
                to = lax.rem(s + start + way * half, SAMP)
                for i in range(SLAB // 128):
                    p = to * (SLAB // 128) + i
                    even, odd = one_row(2 * p), one_row(2 * p + 1)
                    value = field[j, rows_of(c), tile_of(p)]
                    q[j, rows_of(c), tile_of(p)] = (
                        jnp.where(left, pltpu.roll(even, 64, 1), odd) + cap[rows_of(c), tile_of(p)] * value
                    )
                    e[j, rows_of(c), tile_of(p)] = (
                        jnp.where(left, even, pltpu.roll(odd, 64, 1)) + cond[rows_of(c), tile_of(p)] * value
                    )

                @pl.when(to != s)
                def _():
                    remote(
                        q.at[j, rows_of(c), slab_of(to)], bq.at[j, place_of(c, s)], fq_ss.at[j], fq_rs.at[j, c], (d, to)
                    )

            return 0

        lax.fori_loop(0, 2, slabs, 0)
        bq[j, place_of(c, s), :] = q[j, rows_of(c), slab_of(s)]

    def split_charge(j, c):
        await_bytes(bq.at[j, pl.ds(0, CHUNK_ROWS - T)], fq_rs.at[j, c])
        bh[chunk_of(c), :], bl[chunk_of(c), :] = split(bq[j, chunk_of(c), :])

    def slope(c):
        first = jnp.dot(dm[c], bh[...], preferred_element_type=F32)
        second = jnp.dot(dm[c, pl.ds(0, CHUNK_ROWS)], bl[...], preferred_element_type=F32)
        return first[:CHUNK_ROWS] + (first[CHUNK_ROWS:] + second)

    def fold(x):
        x = jnp.sum(x.reshape(-1, T, x.shape[-1]), axis=0)
        return sum(x[:, i * 128 : (i + 1) * 128] for i in range(x.shape[-1] // 128))

    def add_up(parts, terms):
        return tuple(a + fold(b) for a, b in zip(parts, terms, strict=True))

    def send_part(i, parts):
        rows = [jnp.sum(x, axis=0, keepdims=True) for x in parts]
        part[i] = jnp.concatenate(rows + [jnp.zeros((T - len(rows), 128), F32)], axis=0)
        mine = x * 4 + y
        over_square(lambda k: remote(part.at[i], red_s.at[i, mine], rs_ss.at[i], rs_rs.at[i], in_plane(k)))
        red_s[i, mine] = part[i]

    def pass_part(i):
        await_bytes(red_s.at[i, pl.ds(0, SQUARE - 1)], rs_rs.at[i])
        mine = z * 2 + core
        red_d[i, mine] = jnp.sum(red_s[i], axis=0)
        over_square(lambda k: remote(red_d.at[i, mine], red_d.at[i, mine], rd_ss.at[i], rd_rs.at[i], in_line(k)))

    def sums(i):
        await_bytes(red_d.at[i, pl.ds(0, SQUARE - 1)], rd_rs.at[i])
        total = jnp.sum(red_d[i], axis=0)
        return [jnp.sum(total[k : k + 1, :], axis=1, keepdims=True) for k in range(3)]

    zero = jnp.zeros((T, 128), F32)

    loads[0].wait()
    for j in range(2):
        for c in range(CH):
            rbuf[j, c, d] = jnp.zeros((2, T, 128), F32)
    widen(0, 0)
    loads[1].wait()
    over_dom(lambda to: pack(0, 0, to))
    pl.semaphore_wait(barrier, DOM + SAMP - 2 + 9 + 7)
    over_dom(lambda to: send_dom(0, 0, to))

    def early(c, _):
        widen(0, c)
        pack_and_send(0, c)
        return 0

    lax.fori_loop(1, CH, early, 0)

    def share_residual(c, _):
        forward(field.at[0], br, c, fr_ss, fr_rs)
        return 0

    lax.fori_loop(0, CH, share_residual, 0)

    loads[3].wait()

    def halves(row, _):
        high, low = split(w32[row])
        w16[row, :, 0:128] = high
        w16[row, :, 128:256] = low
        return 0

    lax.fori_loop(0, ROWS, halves, 0, unroll=2)
    for i in (2, 4, 5, 6):
        loads[i].wait()

    def first(c, _):
        product(0, c)

        @pl.when(c > 0)
        def _():
            split_charge(0, c - 1)

        return 0

    lax.fori_loop(0, CH, first, 0)
    split_charge(0, CH - 1)

    def slopes(c, _):
        slo[chunk_of(c), :] = slope(c)
        over_samp(
            lambda to: remote(
                slo.at[place_of(c, to)], back.at[rows_of(c), slab_of(s)], back_ss, back_rs.at[c], (d, to)
            )
        )
        back[rows_of(c), slab_of(s)] = slo[place_of(c, s), :]
        return 0

    lax.fori_loop(0, CH, slopes, 0)

    def again(c, _):
        await_bytes(back.at[rows_of(c), pl.ds(0, N - SLAB)], back_rs.at[c])
        field[1, rows_of(c), :] = e[0, rows_of(c), :] + back[rows_of(c), :]
        widen(1, c)
        pack_and_send(1, c)
        return 0

    lax.fori_loop(0, CH, again, 0)

    def share_direct(c, _):
        forward(e.at[0], be.at[0], c, fe_ss.at[0], fe_rs.at[0])
        return 0

    lax.fori_loop(0, CH, share_direct, 0)

    def second(c, _):
        product(1, c)
        forward(e.at[1], be.at[1], c, fe_ss.at[1], fe_rs.at[1])

        @pl.when(c == 0)
        def _():
            await_bytes(br.at[pl.ds(0, ORDER - ORDER // SAMP)], fr_rs)
            await_bytes(be.at[0, pl.ds(0, ORDER - ORDER // SAMP)], fe_rs.at[0])

            def step(i, parts):
                one = slo[chunk_of(i), :] + be[0, chunk_of(i), :]
                z1b[chunk_of(i), :] = one
                start = br[chunk_of(i), :]
                return add_up(parts, (start * start, start * one, one * one))

            send_part(0, lax.fori_loop(0, CH, step, (zero, zero, zero)))

        @pl.when(c > 0)
        def _():
            split_charge(1, c - 1)

        @pl.when(c == 2)
        def _():
            pass_part(0)

        return 0

    lax.fori_loop(0, CH, second, 0)
    square, cross, image = sums(0)
    share = cross / square
    split_charge(1, CH - 1)

    def last_slopes(c, _):
        bq[0, chunk_of(c), :] = slope(c)
        return 0

    lax.fori_loop(0, CH, last_slopes, 0, unroll=4)
    await_bytes(be.at[1, pl.ds(0, ORDER - ORDER // SAMP)], fe_rs.at[1])

    def dots(c, parts):
        one = z1b[chunk_of(c), :]
        two = bq[0, chunk_of(c), :] + be[1, chunk_of(c), :] - share * one
        return add_up(parts, (br[chunk_of(c), :] * two, one * two, two * two))

    send_part(1, lax.fori_loop(0, CH, dots, (zero, zero, zero), unroll=4))
    pass_part(1)

    for j in range(2):
        await_bytes(sbuf.at[j, :, pl.ds(0, DOM - 1)], dom_ss.at[j])
        await_bytes(q.at[j, :, pl.ds(0, N - SLAB)], fq_ss.at[j])
        await_bytes(e.at[j, :, pl.ds(0, N - SLAB)], fe_ss.at[j])
        await_bytes(red_s.at[j, pl.ds(0, SQUARE - 1)], rs_ss.at[j])
    await_bytes(br.at[pl.ds(0, ORDER - ORDER // SAMP)], fr_ss)
    await_bytes(slo.at[pl.ds(0, ORDER - ORDER // SAMP)], back_ss)

    target, gram_cross, gram_second = sums(1)
    determinant = image * gram_second - gram_cross * gram_cross
    weight_first = (gram_second * cross - gram_cross * target) / determinant
    weight_second = (image * target - gram_cross * cross) / determinant

    def finish(c, _):
        residual = field[0, rows_of(c), :]
        out[rows_of(c), :] = weight_first * residual + weight_second * (field[1, rows_of(c), :] - share * residual)
        pltpu.make_async_copy(out.at[rows_of(c)], out_hbm.at[rows_of(c)], out_sem).start()
        return 0

    lax.fori_loop(0, CH, finish, 0)
    for j in range(2):
        await_bytes(red_d.at[j, pl.ds(0, SQUARE - 1)], rd_ss.at[j])
    pltpu.make_async_copy(out, out_hbm, out_sem).wait()


def body(residual, conductance, capacitance, stamps, block_cols, send_blocks):
    anywhere = pl.BlockSpec(memory_space=pl.ANY)
    dma = pltpu.SemaphoreType.DMA
    here = (CH * T, N)
    all_samples = (ORDER, SLAB)
    vmem = pltpu.VMEM
    return pl.pallas_call(
        kernel,
        out_shape=jax.ShapeDtypeStruct(here, F32),
        in_specs=[anywhere] * 7,
        out_specs=anywhere,
        scratch_shapes=[
            pltpu.SMEM((4, ROWS), jnp.int32), pltpu.SMEM((SLOTS, DOM), jnp.int32), vmem(here, F32),
            vmem((2, *here), F32), vmem(here, F32), vmem(here, F32),
            vmem((ROWS, 256, 128), F32), vmem((ROWS, 256, 256), BF16),
            vmem((CH, 2 * CHUNK_ROWS, ORDER), BF16),
            vmem((ROWS, T, 128), F32), vmem((ROWS + SLOTS * DOM, 2 * T, 128), BF16),
            vmem((2, CH, DOM, 2, T, 128), F32), vmem((2, CH, DOM, 2, T, 128), F32),
            vmem((2, *here), F32), vmem((2, *here), F32),
            vmem((2, *all_samples), F32), vmem((2, *all_samples), F32), vmem(all_samples, F32),
            vmem(all_samples, BF16), vmem(all_samples, BF16), vmem(all_samples, F32), vmem(all_samples, F32), vmem(here, F32),
            vmem((2, T, 128), F32), vmem((2, SQUARE, T, 128), F32), vmem((2, SQUARE, T, 128), F32),
            dma((7,)), dma((2,)), dma((2, CH)), dma((2,)), dma((2, CH)), dma((2,)), dma((2,)), dma, dma, dma, dma((CH,)),
            dma((2,)), dma((2,)), dma((2,)), dma((2,)), dma,
        ],
        compiler_params=pltpu.CompilerParams(
            collective_id=0, has_side_effects=True, vmem_limit_bytes=56 * 2**20
        ),
        cost_estimate=pl.CostEstimate(flops=1_200_000_000, bytes_accessed=12_000_000, transcendentals=0),
        name="gmres_step",
    )(
        block_cols.T, send_blocks[0].T, residual, conductance, capacitance,
        stamps.reshape(ROWS, 256, 128), jnp.asarray(derivative_matrix()),
    )


def solution(mesh):
    in_specs = (
        P("samp", "dom"),
        P("samp", "dom"),
        P("samp", "dom"),
        P("dom", None, None, None),
        P("dom", None),
        P("dom", None, None),
    )
    return jax.shard_map(body, mesh=mesh, in_specs=in_specs, out_specs=P("samp", "dom"), check_vma=False)
```
